256 devices in a mesh: merge: 8 (over y, core), grp: 32 (over z, x).
Axes of the slice: x: 4, y: 4, z: 8, core: 2. Of those that a mesh axis runs over, the one named last changes fastest.
Arguments:
- child_vectors: bfloat16 [16, 2048, 2048], P('merge', 'grp'), parts along dimension 0, may hold values from -0.125 to 0.125
- child_values: float32 [32768], P('merge'), parts along dimension 0, may hold values from -2 to 2, as said below
- deflated: int32 [32768], P('merge'), parts along dimension 0, may hold values from 0 to 1, as said below
- order: int32 [32768], P('merge'), parts along dimension 0, may hold values from 0 to 4095, as said below
- coupling: float32 [8], P('merge'), parts along dimension 0, may hold values from 0.5 to 2
Outputs:
- eigenvalues: float32 [32768], P(('merge', 'grp')), parts along dimension 0
- eigenvectors: bfloat16 [32768, 4096], P('merge', 'grp'), parts along dimension 0
The draws below stay inside these ranges and needn't reach their ends.
There are 8 independent parts, one for each index of `merge`. The reference program is written for one: setup_inputs(seed, part) draws one part's arguments, and reference() takes and returns one part's arrays. A program takes and returns all parts, laid end to end along the dimension named above; each array names one. Nothing has to cross between parts.
Inputs may be any that keep to these rules, and one draw needn't show every extreme that they name: `child_values`: within each child (2048 values each) the values ascend; all 4096 values are distinct and any two differ by more than 1.6 / 4096. 1 marks a deflated eigenvalue. Every index appears once: first the indices with deflated 0 in ascending order of child_values, then those with deflated 1 in ascending order of child_values.
All inputs are finite; a program needn't handle non-finite values.
Results may differ from the reference program's by a relative error of at most 0.0034.
Values may be sent and summed in bfloat16 or wider, within the bound.
No kernel may reach another device: no remote copies, remote signals or barrier semaphores. Data moves between devices by JAX's collectives and lax.ppermute only.
A program may use at most 64 MiB of HBM per device.

```python
import jax
import jax.numpy as jnp
from jax import lax

NH = 2048
ITERS = 4


def rank_layout(key):
    full_order = 2 * NH
    shuffle = jax.random.permutation(jax.random.fold_in(key, 101), full_order).astype(jnp.int32)
    first_ranks = jnp.sort(shuffle[:NH])
    second_ranks = jnp.sort(shuffle[NH:])
    ranks = jnp.concatenate([first_ranks, second_ranks])
    dropped = (jax.random.randint(jax.random.fold_in(key, 102), (full_order,), 0, 4) == 0).astype(jnp.int32)
    return (ranks, dropped)


def draw_child_values(key, part):
    ranks, dropped = rank_layout(key)
    key = jax.random.fold_in(key, 3)
    jitter = jax.random.uniform(key, (2 * NH,), jnp.float32)
    spacing = 4.0 / (2 * NH)
    return -2.0 + (ranks.astype(jnp.float32) + 0.2 + 0.6 * jitter) * spacing


def draw_deflated(key, part):
    ranks, dropped = rank_layout(key)
    return dropped


def draw_order(key, part):
    ranks, dropped = rank_layout(key)
    scores = ranks + 2 * NH * dropped
    return jnp.argsort(scores, stable=True).astype(jnp.int32)


def block_levels(stream_key, dims, pieces, smallest, largest):
    def one(dim, parts):
        steps = jax.random.uniform(jax.random.fold_in(jax.random.fold_in(stream_key, 6), dim), (parts,), jnp.float32, smallest / len(pieces), largest / len(pieces))
        return jnp.repeat(jnp.exp(steps), dims[dim] // parts).reshape((-1,) + (1,) * (len(dims) - dim - 1))

    loudness = one(*pieces[0])
    for cut in pieces[1:]:
        loudness = loudness * one(*cut)
    return loudness


def gaussian(stream_key, dims, deviation, limit, split=(), held_as=jnp.bfloat16):
    array = jax.random.normal(stream_key, dims, jnp.float32) * deviation
    if len(split) > 0:
        array = block_levels(stream_key, dims, split, -0.22, 0.18) * array
    return jnp.clip(array, min=-limit, max=limit).astype(held_as)


def setup_inputs(seed: int = 0, part: int = 0) -> dict:
    keys = jax.random.split(jax.random.key(seed), 6)
    part_splits = jax.random.split(jax.random.fold_in(keys[5], part), 6)
    child_vectors = gaussian(part_splits[0], (2, NH, NH), NH ** -0.5, 0.125, ((1, 32),))
    child_values = draw_child_values(jax.random.fold_in(jax.random.fold_in(keys[5], part), 71), part)
    deflated = draw_deflated(jax.random.fold_in(jax.random.fold_in(keys[5], part), 71), part)
    order = draw_order(jax.random.fold_in(jax.random.fold_in(keys[5], part), 71), part)
    coupling = jnp.clip(jax.random.uniform(part_splits[4], (1,), jnp.float32, 0.5, 2.0), 0.5, 2.0)
    return dict(child_vectors=child_vectors, child_values=child_values, deflated=deflated, order=order, coupling=coupling)


margin = 0.05

def secular_roots(indices, values, living, ordering, weights, coupled):
    full_order = values.shape[0]
    position = jnp.zeros((full_order,), jnp.int32).at[ordering].set(jnp.arange(full_order, dtype=jnp.int32))
    nonzero = jnp.sum(living.astype(jnp.int32))
    places = position[indices]
    successor = ordering[jnp.minimum(places + 1, full_order - 1)]
    anchor = values[indices]
    living_rows = living[indices]
    ceiling = jnp.where(places == nonzero - 1, anchor + coupled * jnp.sum(weights), values[successor])
    spacing = ceiling - anchor
    offsets = values[None, :] - anchor[:, None]
    paired = living_rows[:, None] & living[None, :]
    shifts = 0.5 * spacing
    for sweep_index in range(ITERS):
        gapped = jnp.where(paired, offsets - shifts[:, None], 1.0)
        inverse = 1.0 / gapped
        partial_terms = weights[None, :] * inverse
        residue = 1.0 / coupled + lax.optimization_barrier(jnp.sum(partial_terms, axis=1))
        derivative = jnp.where(living_rows, lax.optimization_barrier(jnp.sum(partial_terms * inverse, axis=1)), 1.0)
        shifts = jnp.clip(shifts - residue / derivative, margin * spacing, (1.0 - margin) * spacing)
    return jnp.where(living_rows, shifts, 0.0)

def loewner_logs(indices, shifts, values, living):
    full_order = values.shape[0]
    offsets = values[None, :] - values[indices][:, None]
    diagonal = indices[:, None] == jnp.arange(full_order, dtype=jnp.int32)[None, :]
    paired = living[indices][:, None] & living[None, :]
    numerator = jnp.where(paired, jnp.abs(offsets - shifts[:, None]), 1.0)
    denominator = jnp.where(paired & ~diagonal, jnp.abs(offsets), 1.0)
    return lax.optimization_barrier(jnp.sum(jnp.log(numerator) - jnp.log(denominator), axis=0))

def weights_hat(log_totals, zvector, living, coupled):
    sign_values = jnp.where(zvector >= 0, 1.0, -1.0)
    return jnp.where(living, sign_values * jnp.sqrt(jnp.exp(log_totals) / coupled), 0.0)

def basis_columns(indices, shifts, values, living, hat_weights):
    full_order = values.shape[0]
    offsets = values[:, None] - values[indices][None, :]
    living_cols = living[indices]
    paired = living[:, None] & living_cols[None, :]
    vectors = hat_weights[:, None] / jnp.where(paired, offsets - shifts[None, :], 1.0)
    lengths = jnp.where(living_cols, jnp.sqrt(lax.optimization_barrier(jnp.sum(vectors * vectors, axis=0))), 1.0)
    identity = (jnp.arange(full_order, dtype=jnp.int32)[:, None] == indices[None, :]).astype(values.dtype)
    return jnp.where(living_cols[None, :], vectors / lengths[None, :], identity)

def reference(child_vectors, child_values, deflated, order, coupling):
    half_order = child_vectors.shape[1]
    full_order = 2 * half_order
    living = deflated == 0
    coupled = coupling[0]
    boundary = jnp.concatenate([child_vectors[0, half_order - 1, :], child_vectors[1, 0, :]]).astype(jnp.float32)
    zvector = jnp.where(living, boundary, 0.0)
    weights = zvector * zvector
    indices = jnp.arange(full_order, dtype=jnp.int32)
    shifts = secular_roots(indices, child_values, living, order, weights, coupled)
    eigenvalues = child_values + shifts
    log_totals = loewner_logs(indices, shifts, child_values, living)
    hat_weights = weights_hat(log_totals, zvector, living, coupled)
    merged_basis = basis_columns(indices, shifts, child_values, living, hat_weights).astype(jnp.bfloat16)
    upper_part = jnp.dot(child_vectors[0], merged_basis[:half_order], preferred_element_type=jnp.float32)
    lower_part = jnp.dot(child_vectors[1], merged_basis[half_order:], preferred_element_type=jnp.float32)
    eigenvectors = jnp.concatenate([upper_part, lower_part], axis=0).astype(jnp.bfloat16)
    return (eigenvalues, eigenvectors)
```

```python
import jax
import jax.numpy as jnp
from jax import lax
from jax.experimental import pallas as pl
from jax.experimental.pallas import tpu as pltpu
from jax.sharding import Mesh, PartitionSpec as P

ITERS = 4
MARGIN = 0.05
FAR = 1.0e6
LANES = 128


def column_of(row):
    n = row.shape[1]
    eye = lax.broadcasted_iota(jnp.int32, (n, n), 0) == lax.broadcasted_iota(jnp.int32, (n, n), 1)
    return jnp.sum(jnp.where(eye, row, 0.0), axis=1, keepdims=True)


def row_of(column):
    n = column.shape[0]
    eye = lax.broadcasted_iota(jnp.int32, (n, n), 0) == lax.broadcasted_iota(jnp.int32, (n, n), 1)
    return jnp.sum(jnp.where(eye, column, 0.0), axis=0, keepdims=True)


def roots_kernel(place, rho_ref, edges, values, flags, out, eig, zrow_out, far, weight, dcol, prod):
    member = place[0]
    rho = rho_ref[0]
    full = values.shape[1]
    half_rows = full // 2 // LANES
    last = edges.shape[0] - 1
    lower = edges[last].astype(jnp.float32)
    upper = edges[0].astype(jnp.float32)
    for r in range(half_rows):
        weight[:, r * LANES : (r + 1) * LANES] = lower[r : r + 1, :]
        s = half_rows + r
        weight[:, s * LANES : (s + 1) * LANES] = upper[r : r + 1, :]
    live = flags[...] == 0
    z = jnp.where(live, weight[...], 0.0)
    zrow_out[...] = z
    w = z * z
    weight[...] = w
    total = jnp.sum(w)
    far[...] = jnp.where(live, values[...], FAR)
    own = pl.ds(pl.multiple_of(member * LANES, LANES), LANES)
    own_values = values[:, own]
    own_live = flags[:, own] == 0
    dcol[...] = jnp.broadcast_to(column_of(own_values), (LANES, LANES))
    prod[...] = jnp.ones_like(prod)
    rows = 32
    inv_rho = 1.0 / rho

    def group(g, _):
        di = dcol[pl.ds(pl.multiple_of(g * rows, rows), rows), :][:, :1]
        e = far[...] - di
        gap = jnp.min(jnp.where(e > 0, e, 2.0 * FAR), axis=1, keepdims=True)
        gap = jnp.where(gap > 0.5 * FAR, (di + rho * total) - di, gap)
        delta = 0.5 * gap
        for _ in range(ITERS):
            e = far[...] - di
            inverse = pltpu.reciprocal(e - delta, approx=True)
            term = weight[...] * inverse
            f = inv_rho + jnp.sum(term, axis=1, keepdims=True)
            h = jnp.sum(term * inverse, axis=1, keepdims=True)
            delta = jnp.clip(delta - f / h, MARGIN * gap, (1.0 - MARGIN) * gap)
        dcol[pl.ds(pl.multiple_of(g * rows, rows), rows), :] = jnp.broadcast_to(delta, (rows, LANES))
        return 0

    lax.fori_loop(0, LANES // rows, group, 0)
    own_delta = jnp.where(own_live, row_of(dcol[...][:, :1]), 0.0)
    eig[...] = own_values + own_delta
    dcol[...] = jnp.broadcast_to(column_of(own_delta), (LANES, LANES))
    vcol = column_of(own_values)
    for g in range(0, LANES, rows):
        num = None
        for k in range(0, rows, 8):
            di = vcol[g + k : g + k + 8, :]
            de = dcol[g + k : g + k + 8, :][:, :1]
            e = far[...] - di
            a = e - de
            b = jnp.where(e == 0, 1.0, e)
            num = a if num is None else num * a
            den = b if k == 0 else den * b
        prod[...] = prod[...] * (num * pltpu.reciprocal(den, approx=True))
    p = prod[...]
    p = p[:4] * p[4:]
    p = p[:2] * p[2:]
    p = p[:1] * p[1:]
    for r in range(full // LANES):
        out[0, r : r + 1, :] = p[:, r * LANES : (r + 1) * LANES]
    out[0, full // LANES : full // LANES + 1, :] = own_delta
    block = out[0]
    for s in range(1, out.shape[0]):
        out[s] = block


def vectors_kernel(
    place, rho_ref, parts, values, flags, zrow, own, left, right, far0, far1, out, far, zhat, basis, held, pdi, pde
):
    step = pl.program_id(0)
    x = place[1]
    nx = 4
    share = own.shape[1]
    rho = rho_ref[0]
    full = values.shape[1]
    half = full // 2
    blocks = full // LANES
    per = out.shape[0]

    @pl.when(step == 0)
    def _():
        p = parts[0, :blocks]
        for s in range(1, parts.shape[0]):
            p = p * parts[s, :blocks]
        p = jnp.sqrt(jnp.abs(p) / rho)
        for r in range(blocks):
            zhat[:, r * LANES : (r + 1) * LANES] = p[r : r + 1, :]
        live = flags[...] == 0
        zhat[...] = jnp.where(live, jnp.where(zrow[...] >= 0, zhat[...], -zhat[...]), 0.0)
        far[...] = jnp.where(live, values[...], FAR)

    for k in range(per):
        owner = (step * per + k) * nx + x
        cols = pl.ds(pl.multiple_of(owner * LANES, LANES), LANES)
        pdi[k * LANES : (k + 1) * LANES, :] = jnp.broadcast_to(column_of(values[:, cols]), (LANES, LANES))
        pde[k * LANES : (k + 1) * LANES, :] = jnp.broadcast_to(
            column_of(parts[owner, blocks : blocks + 1, :]), (LANES, LANES)
        )
    rows = 32

    def group(g, _):
        at = pl.ds(pl.multiple_of(g * rows, rows), rows)
        di = pdi[at, :]
        de = pde[at, :]
        acc = jnp.zeros((rows, LANES), jnp.float32)
        for b in range(blocks):
            sl = slice(b * LANES, (b + 1) * LANES)
            v = zhat[:, sl] * pltpu.reciprocal((far[:, sl] - di) - de, approx=True)
            acc = acc + v * v
            held[:, sl] = v
        scale = lax.rsqrt(jnp.sum(acc, axis=1, keepdims=True))
        scale = jnp.broadcast_to(scale, (rows, LANES))
        for b in range(blocks):
            sl = slice(b * LANES, (b + 1) * LANES)
            basis[at, sl] = (held[:, sl] * scale).astype(jnp.bfloat16)
        return 0

    lax.fori_loop(0, per * LANES // rows, group, 0)
    for c in range(2):
        slots = (own.at[c], left.at[c], right.at[c], (far0, far1)[c])
        lhs = jnp.concatenate([slot[...] for slot in slots], axis=0)
        rhs = basis[:, c * half : (c + 1) * half]
        acc = lax.dot_general(lhs, rhs, (((1,), (1,)), ((), ())), preferred_element_type=jnp.float32)
        for k in range(per):
            owner = (step * per + k) * nx + x
            dead = flags[:, pl.ds(pl.multiple_of(owner * LANES, LANES), LANES)] != 0
            mine = owner < blocks // 2 if c == 0 else owner >= blocks // 2
            inner = owner if c == 0 else owner - blocks // 2
            inner = jnp.where(mine, inner, 0)
            for s, slot in enumerate(slots):
                plain = slot[:, pl.ds(pl.multiple_of(inner * LANES, LANES), LANES)].astype(jnp.float32)
                plain = jnp.where(mine, plain, 0.0)
                got = acc[s * share : (s + 1) * share, k * LANES : (k + 1) * LANES]
                source = lax.rem(x + (0, nx - 1, 1, 2)[s], nx)
                out[k, c, pl.ds(pl.multiple_of(source * share, share), share), :] = jnp.where(dead, plain, got).astype(
                    jnp.bfloat16
                )


def local(child_vectors, child_values, deflated, order, coupling):
    del order
    half = child_vectors.shape[2]
    full = 2 * half
    rows = child_vectors.shape[1]
    nz, nx = lax.axis_size("z"), lax.axis_size("x")
    group = nz * nx
    z, x = lax.axis_index("z"), lax.axis_index("x")
    member = z * nx + x
    blocks = full // LANES
    whole = lambda: pl.BlockSpec(memory_space=pltpu.VMEM)
    scalar = lambda: pl.BlockSpec(memory_space=pltpu.SMEM)

    ahead = [(i, (i + 1) % nx) for i in range(nx)]
    back = [(i, (i - 1) % nx) for i in range(nx)]
    left = lax.ppermute(child_vectors, "x", ahead)
    right = lax.ppermute(child_vectors, "x", back)

    place = jnp.stack([member, x]).astype(jnp.int32)
    edge = jnp.where(member == group - 1, child_vectors[0, rows - 1], child_vectors[1, 0])
    edge = jnp.broadcast_to(edge.reshape(1, half // LANES, LANES), (group, half // LANES, LANES))
    edges = lax.all_to_all(edge, ("z", "x"), 0, 0, tiled=True)
    child_values, left, right = lax.optimization_barrier((child_values, left, right))
    opposite = (lax.ppermute(left[0], "x", ahead), lax.ppermute(right[1], "x", back))
    values = child_values.reshape(1, full)
    flags = deflated.reshape(1, full)
    parts, eig, zrow = pl.pallas_call(
        roots_kernel,
        out_shape=(
            jax.ShapeDtypeStruct((group, blocks + 8, LANES), jnp.float32),
            jax.ShapeDtypeStruct((1, LANES), jnp.float32),
            jax.ShapeDtypeStruct((1, full), jnp.float32),
        ),
        in_specs=[scalar(), scalar(), whole(), whole(), whole()],
        out_specs=(whole(), whole(), whole()),
        scratch_shapes=[
            pltpu.VMEM((1, full), jnp.float32),
            pltpu.VMEM((1, full), jnp.float32),
            pltpu.VMEM((LANES, LANES), jnp.float32),
            pltpu.VMEM((8, full), jnp.float32),
        ],
        compiler_params=pltpu.CompilerParams(vmem_limit_bytes=32 * 1024 * 1024),
        name="roots",
    )(place, coupling, edges, values, flags)
    parts = lax.all_to_all(parts, ("z", "x"), 0, 0, tiled=True)
    per = 2
    produced = pl.pallas_call(
        vectors_kernel,
        grid=(nz // per,),
        out_shape=jax.ShapeDtypeStruct((nz, 2, nx * rows, LANES), jnp.bfloat16),
        in_specs=[scalar(), scalar()] + [whole()] * 9,
        out_specs=pl.BlockSpec((per, 2, nx * rows, LANES), lambda i: (i, 0, 0, 0)),
        scratch_shapes=[
            pltpu.VMEM((1, full), jnp.float32),
            pltpu.VMEM((1, full), jnp.float32),
            pltpu.VMEM((per * LANES, full), jnp.bfloat16),
            pltpu.VMEM((32, full), jnp.float32),
            pltpu.VMEM((per * LANES, LANES), jnp.float32),
            pltpu.VMEM((per * LANES, LANES), jnp.float32),
        ],
        compiler_params=pltpu.CompilerParams(vmem_limit_bytes=40 * 1024 * 1024),
        name="vectors",
    )(place, coupling, parts, values, flags, zrow, child_vectors, left, right, *opposite)
    returned = lax.all_to_all(produced, "z", 0, 0, tiled=True)
    eigenvectors = returned.transpose(1, 0, 2, 3).reshape(full, LANES)
    return eig.reshape(LANES), eigenvectors


def solution(mesh):
    inner = Mesh(mesh.devices.reshape(mesh.devices.shape[0], -1, 4), ("merge", "z", "x"))
    grp = ("z", "x")
    in_specs = (P("merge", grp, None), P("merge"), P("merge"), P("merge"), P("merge"))
    out_specs = (P(("merge",) + grp), P("merge", grp))
    return jax.shard_map(local, mesh=inner, in_specs=in_specs, out_specs=out_specs, check_vma=False)
```

```python
import functools

import jax
import jax.numpy as jnp
from jax import lax
from jax.experimental import pallas as pl
from jax.experimental.pallas import tpu as pltpu
from jax.sharding import Mesh, PartitionSpec as P

ITERS = 4
MARGIN = 0.05
FAR = 1.0e6
LANES = 128


def column_of(row):
    n = row.shape[1]
    eye = lax.broadcasted_iota(jnp.int32, (n, n), 0) == lax.broadcasted_iota(jnp.int32, (n, n), 1)
    return jnp.sum(jnp.where(eye, row, 0.0), axis=1, keepdims=True)


def row_of(column):
    n = column.shape[0]
    eye = lax.broadcasted_iota(jnp.int32, (n, n), 0) == lax.broadcasted_iota(jnp.int32, (n, n), 1)
    return jnp.sum(jnp.where(eye, column, 0.0), axis=0, keepdims=True)


def roots_kernel(place, rho_ref, edges, values, flags, out, eig, zrow_out, far, weight, dist, pdi, pde, prod):
    member = place[0]
    rho = rho_ref[0]
    full = values.shape[1]
    blocks = full // LANES
    half_rows = blocks // 2
    last = edges.shape[0] - 1
    halves = (edges[last].astype(jnp.float32), edges[0].astype(jnp.float32))
    for b in range(blocks):
        zrow_out[:, b * LANES : (b + 1) * LANES] = halves[b // half_rows][b % half_rows : b % half_rows + 1, :]
    live = flags[...] == 0
    z = jnp.where(live, zrow_out[...], 0.0)
    zrow_out[...] = z
    total = rho * jnp.sum(z * z)
    weight[...] = jnp.broadcast_to(z * z, weight.shape)
    far[...] = jnp.broadcast_to(jnp.where(live, values[...], FAR), far.shape)
    own = pl.ds(pl.multiple_of(member * LANES, LANES), LANES)
    own_values = values[:, own]
    own_live = flags[:, own] == 0
    pdi[...] = jnp.broadcast_to(column_of(own_values), (LANES, LANES))
    inv_rho = 1.0 / rho
    depth = 8
    tiles = LANES // 8

    def spread(column):
        return jnp.broadcast_to(column, (8, LANES))

    gap = []
    for g in range(0, tiles, depth):
        di = [pdi[8 * (g + r) : 8 * (g + r) + 8, :] for r in range(depth)]
        low = [jnp.full((8, LANES), 2.0 * FAR, jnp.float32) for _ in range(depth)]
        for b in range(blocks):
            sl = slice(b * LANES, (b + 1) * LANES)
            d = far[:, sl]
            for r in range(depth):
                e = d - di[r]
                dist[8 * (g + r) : 8 * (g + r) + 8, sl] = e
                low[r] = jnp.minimum(low[r], jnp.where(e > 0, e, 2.0 * FAR))
        for r in range(depth):
            least = spread(jnp.min(low[r], axis=1, keepdims=True))
            gap.append(jnp.where(least > 0.5 * FAR, (di[r] + total) - di[r], least))
    for r in range(tiles):
        pdi[8 * r : 8 * r + 8, :] = gap[r]
        pde[8 * r : 8 * r + 8, :] = 0.5 * gap[r]

    def sweep(_, carry):
        for g in range(0, tiles, depth):
            de = [pde[8 * (g + r) : 8 * (g + r) + 8, :] for r in range(depth)]
            f = [jnp.zeros((8, LANES), jnp.float32) for _ in range(depth)]
            h = [jnp.zeros((8, LANES), jnp.float32) for _ in range(depth)]
            for b in range(blocks):
                sl = slice(b * LANES, (b + 1) * LANES)
                w = weight[:, sl]
                for r in range(depth):
                    inverse = pltpu.reciprocal(dist[8 * (g + r) : 8 * (g + r) + 8, sl] - de[r], approx=True)
                    term = w * inverse
                    f[r] = f[r] + term
                    h[r] = h[r] + term * inverse
            for r in range(depth):
                top = inv_rho + spread(jnp.sum(f[r], axis=1, keepdims=True))
                slope = spread(jnp.sum(h[r], axis=1, keepdims=True))
                gp = pdi[8 * (g + r) : 8 * (g + r) + 8, :]
                pde[8 * (g + r) : 8 * (g + r) + 8, :] = jnp.clip(de[r] - top / slope, MARGIN * gp, (1.0 - MARGIN) * gp)
        return carry

    lax.fori_loop(0, ITERS, sweep, 0, unroll=True)
    own_delta = jnp.where(own_live, row_of(pde[...][:, :1]), 0.0)
    eig[...] = own_values + own_delta
    pde[...] = jnp.broadcast_to(column_of(own_delta), (LANES, LANES))
    for b in range(blocks):
        sl = slice(b * LANES, (b + 1) * LANES)
        p = None
        for g in range(0, tiles, 4):
            num = den = None
            for r in range(g, g + 4):
                e = dist[8 * r : 8 * r + 8, sl]
                a = e - pde[8 * r : 8 * r + 8, :]
                c = jnp.where(e == 0, 1.0, e)
                num = a if num is None else num * a
                den = c if den is None else den * c
            ratio = num * pltpu.reciprocal(den, approx=True)
            p = ratio if p is None else p * ratio
        prod[:, sl] = p
    p = prod[...]
    p = p[:4] * p[4:]
    p = p[:2] * p[2:]
    p = p[:1] * p[1:]
    for b in range(blocks):
        out[b : b + 1, :] = p[:, b * LANES : (b + 1) * LANES]
    out[blocks : blocks + 1, :] = own_delta
    out[blocks + 1 :, :] = jnp.zeros((out.shape[0] - blocks - 1, LANES), jnp.float32)


def vectors_kernel(offsets, place, rho_ref, parts, values, flags, *refs):
    first = len(refs) == 14
    if first:
        zrow, own, left, right, far0, far1, *outs, zhat, far = refs[:-4]
    else:
        zhat, far, own, left, right, far0, far1, *outs = refs[:-4]
    basis, held, pdi, pde = refs[-4:]
    z, x = place[1], place[2]
    nz, nx = 8, 4
    share = own.shape[1]
    full = values.shape[1]
    half = full // 2
    blocks = full // LANES

    if first:
        p = parts[0, :blocks]
        for s in range(1, parts.shape[0]):
            p = p * parts[s, :blocks]
        p = jnp.sqrt(jnp.abs(p) / rho_ref[0])
        for r in range(blocks):
            zhat[:, r * LANES : (r + 1) * LANES] = jnp.broadcast_to(p[r : r + 1, :], (8, LANES))
        live = flags[...] == 0
        live8 = jnp.broadcast_to(flags[...], far.shape) == 0
        signed = jnp.where(jnp.broadcast_to(zrow[...], far.shape) >= 0, zhat[...], -zhat[...])
        zhat[...] = jnp.where(live8, signed, 0.0)
        far[...] = jnp.broadcast_to(jnp.where(live, values[...], FAR), far.shape)

    places = [lax.rem(z + offset, nz) for offset in offsets]
    owners = [at * nx + x for at in places]
    for k, owner in enumerate(owners):
        cols = pl.ds(pl.multiple_of(owner * LANES, LANES), LANES)
        pdi[k * LANES : (k + 1) * LANES, :] = jnp.broadcast_to(column_of(values[:, cols]), (LANES, LANES))
        pde[k * LANES : (k + 1) * LANES, :] = jnp.broadcast_to(
            column_of(parts[places[k], blocks : blocks + 1, :]), (LANES, LANES)
        )
    depth = 8

    def group(g):
        base = g * 8 * depth
        di = [pdi[pl.ds(base + 8 * r, 8), :] for r in range(depth)]
        de = [pde[pl.ds(base + 8 * r, 8), :] for r in range(depth)]
        acc = [jnp.zeros((8, LANES), jnp.float32) for _ in range(depth)]
        for b in range(blocks):
            sl = slice(b * LANES, (b + 1) * LANES)
            d, zh = far[:, sl], zhat[:, sl]
            for r in range(depth):
                v = zh * pltpu.reciprocal((d - di[r]) - de[r], approx=True)
                acc[r] = acc[r] + v * v
                held[8 * r : 8 * r + 8, sl] = v
        scale = [lax.rsqrt(jnp.sum(a, axis=1, keepdims=True)) for a in acc]
        scale = [jnp.broadcast_to(a, (8, LANES)) for a in scale]
        for b in range(blocks):
            sl = slice(b * LANES, (b + 1) * LANES)
            for r in range(0, depth, 2):
                u = [held[8 * t : 8 * t + 8, sl] * scale[t] for t in (r, r + 1)]
                basis[pl.ds(base + 8 * r, 16), sl] = jnp.concatenate(u, axis=0).astype(jnp.bfloat16)

    for g in range(len(offsets) * LANES // (8 * depth)):
        group(g)
    for c in range(2):
        slots = (own.at[c], left.at[c], right.at[c], (far0, far1)[c])
        lhs = jnp.concatenate([slot[...] for slot in slots], axis=0)
        rhs = basis[:, c * half : (c + 1) * half]
        acc = lax.dot_general(lhs, rhs, (((1,), (1,)), ((), ())), preferred_element_type=jnp.float32)
        for k, owner in enumerate(owners):
            dead = flags[:, pl.ds(pl.multiple_of(owner * LANES, LANES), LANES)] != 0
            mine = owner < blocks // 2 if c == 0 else owner >= blocks // 2
            inner = jnp.where(mine, owner if c == 0 else owner - blocks // 2, 0)
            for s, slot in enumerate(slots):
                plain = slot[:, pl.ds(pl.multiple_of(inner * LANES, LANES), LANES)].astype(jnp.float32)
                plain = jnp.where(mine, plain, 0.0)
                got = acc[s * share : (s + 1) * share, k * LANES : (k + 1) * LANES]
                source = lax.rem(x + (0, nx - 1, 1, 2)[s], nx)
                outs[k][c, pl.ds(pl.multiple_of(source * share, share), share), :] = jnp.where(dead, plain, got).astype(
                    jnp.bfloat16
                )


def assemble_kernel(order, place, *refs):
    pieces, out, sems = refs[:-2], refs[-2], refs[-1]
    nz = len(pieces)
    copies = []
    for k, (offset, piece) in enumerate(zip(order, pieces)):
        source = lax.rem(place[1] + nz - offset, nz)
        copy = pltpu.make_async_copy(piece, out.at[:, source], sems.at[k])
        copy.start()
        copies.append(copy)
    for copy in copies:
        copy.wait()


def local(child_vectors, child_values, deflated, order, coupling):
    del order
    half = child_vectors.shape[2]
    full = 2 * half
    rows = child_vectors.shape[1]
    nz, nx = lax.axis_size("z"), lax.axis_size("x")
    group = nz * nx
    z, x = lax.axis_index("z"), lax.axis_index("x")
    member = z * nx + x
    blocks = full // LANES
    whole = lambda: pl.BlockSpec(memory_space=pltpu.VMEM)
    scalar = lambda: pl.BlockSpec(memory_space=pltpu.SMEM)

    ahead = [(i, (i + 1) % nx) for i in range(nx)]
    back = [(i, (i - 1) % nx) for i in range(nx)]
    left = lax.ppermute(child_vectors, "x", ahead)
    right = lax.ppermute(child_vectors, "x", back)

    place = jnp.stack([member, z, x]).astype(jnp.int32)
    edge = jnp.where(member == group - 1, child_vectors[0, rows - 1], child_vectors[1, 0])
    edge = jnp.broadcast_to(edge.reshape(1, half // LANES, LANES), (group, half // LANES, LANES))
    edges = lax.all_to_all(edge, ("z", "x"), 0, 0, tiled=True)
    child_values, left, right = lax.optimization_barrier((child_values, left, right))
    values = child_values.reshape(1, full)
    flags = deflated.reshape(1, full)
    block, eig, zrow = pl.pallas_call(
        roots_kernel,
        out_shape=(
            jax.ShapeDtypeStruct((blocks + 8, LANES), jnp.float32),
            jax.ShapeDtypeStruct((1, LANES), jnp.float32),
            jax.ShapeDtypeStruct((1, full), jnp.float32),
        ),
        in_specs=[scalar(), scalar(), whole(), whole(), whole()],
        out_specs=(whole(), whole(), whole()),
        scratch_shapes=[
            pltpu.VMEM((8, full), jnp.float32),
            pltpu.VMEM((8, full), jnp.float32),
            pltpu.VMEM((LANES, full), jnp.float32),
            pltpu.VMEM((LANES, LANES), jnp.float32),
            pltpu.VMEM((LANES, LANES), jnp.float32),
            pltpu.VMEM((8, full), jnp.float32),
        ],
        compiler_params=pltpu.CompilerParams(vmem_limit_bytes=32 * 1024 * 1024),
        name="roots",
    )(place, coupling, edges, values, flags)
    others = [lax.ppermute(block, "x", [(i, (i + k) % nx) for i in range(nx)]) for k in (2, 1, 3)]
    left, right, *others = lax.optimization_barrier((left, right, *others))
    opposite = (lax.ppermute(left[0], "x", ahead), lax.ppermute(right[1], "x", back))
    product = block
    for other in others:
        product = product * other
    lines = lax.broadcasted_iota(jnp.int32, block.shape, 0)
    parts = jnp.broadcast_to(jnp.where(lines < blocks, product, block), (nz,) + block.shape)
    parts = lax.all_to_all(parts, "z", 0, 0, tiled=True)
    order = (4, 5, 3, 6, 2, 7, 1, 0)
    piece = jax.ShapeDtypeStruct((2, nx * rows, LANES), jnp.bfloat16)
    wide = jax.ShapeDtypeStruct((8, full), jnp.float32)
    held = (zrow,)
    pieces = []
    for at in range(0, nz, 2):
        pair = order[at : at + 2]
        extra = (wide, wide) if at == 0 else ()
        *made, = pl.pallas_call(
            functools.partial(vectors_kernel, pair),
            out_shape=(piece,) * 2 + extra,
            in_specs=[scalar(), scalar()] + [whole()] * (8 + len(held)),
            out_specs=(whole(),) * (2 + len(extra)),
            scratch_shapes=[
                pltpu.VMEM((2 * LANES, full), jnp.bfloat16),
                pltpu.VMEM((64, full), jnp.float32),
                pltpu.VMEM((2 * LANES, LANES), jnp.float32),
                pltpu.VMEM((2 * LANES, LANES), jnp.float32),
            ],
            compiler_params=pltpu.CompilerParams(vmem_limit_bytes=24 * 1024 * 1024),
            name="vectors",
        )(place, coupling, parts, values, flags, *held, child_vectors, left, right, *opposite)
        if at == 0:
            held = tuple(made[2:])
        for offset, block in zip(pair, made[:2]):
            if offset:
                block = lax.ppermute(block, "z", [(i, (i + offset) % nz) for i in range(nz)])
            pieces.append(block)
    eigenvectors = pl.pallas_call(
        functools.partial(assemble_kernel, order),
        out_shape=jax.ShapeDtypeStruct((2, nz, nx * rows, LANES), jnp.bfloat16),
        in_specs=[scalar()] + [whole()] * nz,
        out_specs=pl.BlockSpec(memory_space=pl.ANY),
        scratch_shapes=[pltpu.SemaphoreType.DMA((nz,))],
        name="assemble",
    )(place, *pieces).reshape(full, LANES)
    return eig.reshape(LANES), eigenvectors


def solution(mesh):
    inner = Mesh(mesh.devices.reshape(mesh.devices.shape[0], -1, 4), ("merge", "z", "x"))
    grp = ("z", "x")
    in_specs = (P("merge", grp, None), P("merge"), P("merge"), P("merge"), P("merge"))
    out_specs = (P(("merge",) + grp), P("merge", grp))
    return jax.shard_map(local, mesh=inner, in_specs=in_specs, out_specs=out_specs, check_vma=False)
```

```python
import functools

import jax
import jax.numpy as jnp
from jax import lax
from jax.experimental import pallas as pl
from jax.experimental.pallas import tpu as pltpu
from jax.sharding import Mesh, PartitionSpec as P

ITERS = 4
MARGIN = 0.05
FAR = 1.0e6
LANES = 128


def column_of(row):
    n = row.shape[1]
    eye = lax.broadcasted_iota(jnp.int32, (n, n), 0) == lax.broadcasted_iota(jnp.int32, (n, n), 1)
    return jnp.sum(jnp.where(eye, row, 0.0), axis=1, keepdims=True)


def row_of(column):
    n = column.shape[0]
    eye = lax.broadcasted_iota(jnp.int32, (n, n), 0) == lax.broadcasted_iota(jnp.int32, (n, n), 1)
    return jnp.sum(jnp.where(eye, column, 0.0), axis=0, keepdims=True)


def roots_kernel(place, rho_ref, edges, values, flags, out, eig, zrow_out, far, weight, dist, pdi, pde, prod):
    member = place[0]
    rho = rho_ref[0]
    full = values.shape[1]
    blocks = full // LANES
    half_rows = blocks // 2
    last = edges.shape[0] - 1
    halves = (edges[last].astype(jnp.float32), edges[0].astype(jnp.float32))
    for b in range(blocks):
        zrow_out[:, b * LANES : (b + 1) * LANES] = halves[b // half_rows][b % half_rows : b % half_rows + 1, :]
    live = flags[...] == 0
    z = jnp.where(live, zrow_out[...], 0.0)
    zrow_out[...] = z
    total = rho * jnp.sum(z * z)
    weight[...] = jnp.broadcast_to(z * z, weight.shape)
    far[...] = jnp.broadcast_to(jnp.where(live, values[...], FAR), far.shape)
    own = pl.ds(pl.multiple_of(member * LANES, LANES), LANES)
    own_values = values[:, own]
    own_live = flags[:, own] == 0
    pdi[...] = jnp.broadcast_to(column_of(own_values), (LANES, LANES))
    inv_rho = 1.0 / rho
    depth = 8
    tiles = LANES // 8

    def spread(column):
        return jnp.broadcast_to(column, (8, LANES))

    gap = []
    for g in range(0, tiles, depth):
        di = [pdi[8 * (g + r) : 8 * (g + r) + 8, :] for r in range(depth)]
        low = [jnp.full((8, LANES), 2.0 * FAR, jnp.float32) for _ in range(depth)]
        for b in range(blocks):
            sl = slice(b * LANES, (b + 1) * LANES)
            d = far[:, sl]
            for r in range(depth):
                e = d - di[r]
                dist[8 * (g + r) : 8 * (g + r) + 8, sl] = e
                low[r] = jnp.minimum(low[r], jnp.where(e > 0, e, 2.0 * FAR))
        for r in range(depth):
            least = spread(jnp.min(low[r], axis=1, keepdims=True))
            gap.append(jnp.where(least > 0.5 * FAR, (di[r] + total) - di[r], least))
    for r in range(tiles):
        pdi[8 * r : 8 * r + 8, :] = gap[r]
        pde[8 * r : 8 * r + 8, :] = 0.5 * gap[r]

    def sweep(_, carry):
        for g in range(0, tiles, depth):
            de = [pde[8 * (g + r) : 8 * (g + r) + 8, :] for r in range(depth)]
            f = [jnp.zeros((8, LANES), jnp.float32) for _ in range(depth)]
            h = [jnp.zeros((8, LANES), jnp.float32) for _ in range(depth)]
            for b in range(blocks):
                sl = slice(b * LANES, (b + 1) * LANES)
                w = weight[:, sl]
                for r in range(depth):
                    inverse = pltpu.reciprocal(dist[8 * (g + r) : 8 * (g + r) + 8, sl] - de[r], approx=True)
                    term = w * inverse
                    f[r] = f[r] + term
                    h[r] = h[r] + term * inverse
            for r in range(depth):
                top = inv_rho + spread(jnp.sum(f[r], axis=1, keepdims=True))
                slope = spread(jnp.sum(h[r], axis=1, keepdims=True))
                gp = pdi[8 * (g + r) : 8 * (g + r) + 8, :]
                pde[8 * (g + r) : 8 * (g + r) + 8, :] = jnp.clip(de[r] - top / slope, MARGIN * gp, (1.0 - MARGIN) * gp)
        return carry

    lax.fori_loop(0, ITERS, sweep, 0, unroll=True)
    own_delta = jnp.where(own_live, row_of(pde[...][:, :1]), 0.0)
    eig[...] = own_values + own_delta
    pde[...] = jnp.broadcast_to(column_of(own_delta), (LANES, LANES))
    for b in range(blocks):
        sl = slice(b * LANES, (b + 1) * LANES)
        p = None
        for g in range(0, tiles, 4):
            num = den = None
            for r in range(g, g + 4):
                e = dist[8 * r : 8 * r + 8, sl]
                a = e - pde[8 * r : 8 * r + 8, :]
                c = jnp.where(e == 0, 1.0, e)
                num = a if num is None else num * a
                den = c if den is None else den * c
            ratio = num * pltpu.reciprocal(den, approx=True)
            p = ratio if p is None else p * ratio
        prod[:, sl] = p
    p = prod[...]
    p = p[:4] * p[4:]
    p = p[:2] * p[2:]
    p = p[:1] * p[1:]
    for b in range(blocks):
        out[b : b + 1, :] = p[:, b * LANES : (b + 1) * LANES]
    out[blocks : blocks + 1, :] = own_delta
    out[blocks + 1 :, :] = jnp.zeros((out.shape[0] - blocks - 1, LANES), jnp.float32)


def vectors_kernel(offsets, first, place, rho_ref, parts, values, flags, *refs):
    if first:
        zrow, own, left, right, far0, far1, *outs, zhat, far = refs[:-4]
    else:
        zhat, far, own, left, right, far0, far1, *outs = refs[:-4]
    basis, held, pdi, pde = refs[-4:]
    z, x = place[1], place[2]
    nz, nx = 8, 4
    share = own.shape[1]
    full = values.shape[1]
    half = full // 2
    blocks = full // LANES

    if first:
        p = parts[0, :blocks]
        for s in range(1, parts.shape[0]):
            p = p * parts[s, :blocks]
        p = jnp.sqrt(jnp.abs(p) / rho_ref[0])
        for r in range(blocks):
            zhat[:, r * LANES : (r + 1) * LANES] = jnp.broadcast_to(p[r : r + 1, :], (8, LANES))
        live = flags[...] == 0
        live8 = jnp.broadcast_to(flags[...], far.shape) == 0
        signed = jnp.where(jnp.broadcast_to(zrow[...], far.shape) >= 0, zhat[...], -zhat[...])
        zhat[...] = jnp.where(live8, signed, 0.0)
        far[...] = jnp.broadcast_to(jnp.where(live, values[...], FAR), far.shape)

    places = [lax.rem(z + offset, nz) for offset in offsets]
    owners = [at * nx + x for at in places]
    for k, owner in enumerate(owners):
        cols = pl.ds(pl.multiple_of(owner * LANES, LANES), LANES)
        pdi[k * LANES : (k + 1) * LANES, :] = jnp.broadcast_to(column_of(values[:, cols]), (LANES, LANES))
        pde[k * LANES : (k + 1) * LANES, :] = jnp.broadcast_to(
            column_of(parts[places[k], blocks : blocks + 1, :]), (LANES, LANES)
        )
    depth = 8

    def group(g):
        base = g * 8 * depth
        di = [pdi[pl.ds(base + 8 * r, 8), :] for r in range(depth)]
        de = [pde[pl.ds(base + 8 * r, 8), :] for r in range(depth)]
        acc = [jnp.zeros((8, LANES), jnp.float32) for _ in range(depth)]
        for b in range(blocks):
            sl = slice(b * LANES, (b + 1) * LANES)
            d, zh = far[:, sl], zhat[:, sl]
            for r in range(depth):
                v = zh * pltpu.reciprocal((d - di[r]) - de[r], approx=True)
                acc[r] = acc[r] + v * v
                held[8 * r : 8 * r + 8, sl] = v
        scale = [lax.rsqrt(jnp.sum(a, axis=1, keepdims=True)) for a in acc]
        scale = [jnp.broadcast_to(a, (8, LANES)) for a in scale]
        for b in range(blocks):
            sl = slice(b * LANES, (b + 1) * LANES)
            for r in range(0, depth, 2):
                u = [held[8 * t : 8 * t + 8, sl] * scale[t] for t in (r, r + 1)]
                basis[pl.ds(base + 8 * r, 16), sl] = jnp.concatenate(u, axis=0).astype(jnp.bfloat16)

    for g in range(len(offsets) * LANES // (8 * depth)):
        group(g)
    for c in range(2):
        slots = (own.at[c], left.at[c], right.at[c], (far0, far1)[c])
        lhs = jnp.concatenate([slot[...] for slot in slots], axis=0)
        rhs = basis[:, c * half : (c + 1) * half]
        acc = lax.dot_general(lhs, rhs, (((1,), (1,)), ((), ())), preferred_element_type=jnp.float32)
        for k, owner in enumerate(owners):
            dead = flags[:, pl.ds(pl.multiple_of(owner * LANES, LANES), LANES)] != 0
            mine = owner < blocks // 2 if c == 0 else owner >= blocks // 2
            inner = jnp.where(mine, owner if c == 0 else owner - blocks // 2, 0)
            for s, slot in enumerate(slots):
                plain = slot[:, pl.ds(pl.multiple_of(inner * LANES, LANES), LANES)].astype(jnp.float32)
                plain = jnp.where(mine, plain, 0.0)
                got = acc[s * share : (s + 1) * share, k * LANES : (k + 1) * LANES]
                source = lax.rem(x + (0, nx - 1, 1, 2)[s], nx)
                outs[k][c, pl.ds(pl.multiple_of(source * share, share), share), :] = jnp.where(dead, plain, got).astype(
                    jnp.bfloat16
                )


def local(child_vectors, child_values, deflated, order, coupling):
    del order
    half = child_vectors.shape[2]
    full = 2 * half
    rows = child_vectors.shape[1]
    nz, nx = lax.axis_size("z"), lax.axis_size("x")
    group = nz * nx
    z, x = lax.axis_index("z"), lax.axis_index("x")
    member = z * nx + x
    blocks = full // LANES
    whole = lambda: pl.BlockSpec(memory_space=pltpu.VMEM)
    scalar = lambda: pl.BlockSpec(memory_space=pltpu.SMEM)

    ahead = [(i, (i + 1) % nx) for i in range(nx)]
    back = [(i, (i - 1) % nx) for i in range(nx)]
    left = lax.ppermute(child_vectors, "x", ahead)
    right = lax.ppermute(child_vectors, "x", back)

    place = jnp.stack([member, z, x]).astype(jnp.int32)
    edge = jnp.where(member == group - 1, child_vectors[0, rows - 1], child_vectors[1, 0])
    edge = jnp.broadcast_to(edge.reshape(1, half // LANES, LANES), (group, half // LANES, LANES))
    edges = lax.all_to_all(edge, ("z", "x"), 0, 0, tiled=True)
    child_values, left, right = lax.optimization_barrier((child_values, left, right))
    values = child_values.reshape(1, full)
    flags = deflated.reshape(1, full)
    block, eig, zrow = pl.pallas_call(
        roots_kernel,
        out_shape=(
            jax.ShapeDtypeStruct((blocks + 8, LANES), jnp.float32),
            jax.ShapeDtypeStruct((1, LANES), jnp.float32),
            jax.ShapeDtypeStruct((1, full), jnp.float32),
        ),
        in_specs=[scalar(), scalar(), whole(), whole(), whole()],
        out_specs=(whole(), whole(), whole()),
        scratch_shapes=[
            pltpu.VMEM((8, full), jnp.float32),
            pltpu.VMEM((8, full), jnp.float32),
            pltpu.VMEM((LANES, full), jnp.float32),
            pltpu.VMEM((LANES, LANES), jnp.float32),
            pltpu.VMEM((LANES, LANES), jnp.float32),
            pltpu.VMEM((8, full), jnp.float32),
        ],
        compiler_params=pltpu.CompilerParams(vmem_limit_bytes=32 * 1024 * 1024),
        name="roots",
    )(place, coupling, edges, values, flags)
    others = [lax.ppermute(block, "x", [(i, (i + k) % nx) for i in range(nx)]) for k in (2, 1, 3)]
    left, right, *others = lax.optimization_barrier((left, right, *others))
    opposite = (lax.ppermute(left[0], "x", ahead), lax.ppermute(right[1], "x", back))
    product = block
    for other in others:
        product = product * other
    lines = lax.broadcasted_iota(jnp.int32, block.shape, 0)
    parts = jnp.broadcast_to(jnp.where(lines < blocks, product, block), (nz,) + block.shape)
    parts = lax.all_to_all(parts, "z", 0, 0, tiled=True)
    calls = ((4,), (5, 3), (6, 2), (7, 1), (0,))
    order = sum(calls, ())
    piece = jax.ShapeDtypeStruct((2, nx * rows, LANES), jnp.bfloat16)
    wide = jax.ShapeDtypeStruct((8, full), jnp.float32)
    held = (zrow,)
    pieces = []
    for at, some in enumerate(calls):
        wait = {3: 0, 4: 1}.get(at)
        if wait is not None:
            pieces[wait], *held = lax.optimization_barrier((pieces[wait], *held))
        extra = (wide, wide) if at == 0 else ()
        *made, = pl.pallas_call(
            functools.partial(vectors_kernel, some, at == 0),
            out_shape=(piece,) * len(some) + extra,
            in_specs=[scalar(), scalar()] + [whole()] * (8 + len(held)),
            out_specs=(whole(),) * (len(some) + len(extra)),
            scratch_shapes=[
                pltpu.VMEM((len(some) * LANES, full), jnp.bfloat16),
                pltpu.VMEM((64, full), jnp.float32),
                pltpu.VMEM((len(some) * LANES, LANES), jnp.float32),
                pltpu.VMEM((len(some) * LANES, LANES), jnp.float32),
            ],
            compiler_params=pltpu.CompilerParams(vmem_limit_bytes=24 * 1024 * 1024),
            name="vectors",
        )(place, coupling, parts, values, flags, *held, child_vectors, left, right, *opposite)
        if at == 0:
            held = tuple(made[len(some) :])
        for offset, block in zip(some, made):
            if offset:
                block = lax.ppermute(block, "z", [(i, (i + offset) % nz) for i in range(nz)])
            pieces.append(block)
    eigenvectors = jnp.zeros((2, nz, nx * rows, LANES), jnp.bfloat16)
    for offset, block in zip(order, pieces):
        source = lax.rem(z + nz - offset, nz)
        eigenvectors = lax.dynamic_update_slice(eigenvectors, block[:, None], (0, source, 0, 0))
    eigenvectors = eigenvectors.reshape(full, LANES)
    return eig.reshape(LANES), eigenvectors


def solution(mesh):
    inner = Mesh(mesh.devices.reshape(mesh.devices.shape[0], -1, 4), ("merge", "z", "x"))
    grp = ("z", "x")
    in_specs = (P("merge", grp, None), P("merge"), P("merge"), P("merge"), P("merge"))
    out_specs = (P(("merge",) + grp), P("merge", grp))
    return jax.shard_map(local, mesh=inner, in_specs=in_specs, out_specs=out_specs, check_vma=False)
```

```python
import functools

import jax
import jax.numpy as jnp
from jax import lax
from jax.experimental import pallas as pl
from jax.experimental.pallas import tpu as pltpu
from jax.sharding import Mesh, PartitionSpec as P

ITERS = 4
MARGIN = 0.05
FAR = 1.0e6
LANES = 128


def column_of(row):
    n = row.shape[1]
    eye = lax.broadcasted_iota(jnp.int32, (n, n), 0) == lax.broadcasted_iota(jnp.int32, (n, n), 1)
    return jnp.sum(jnp.where(eye, row, 0.0), axis=1, keepdims=True)


def row_of(column):
    n = column.shape[0]
    eye = lax.broadcasted_iota(jnp.int32, (n, n), 0) == lax.broadcasted_iota(jnp.int32, (n, n), 1)
    return jnp.sum(jnp.where(eye, column, 0.0), axis=0, keepdims=True)


def roots_kernel(place, rho_ref, edges, values, flags, out, eig, zrow_out, far, weight, dist, pdi, pde, prod):
    member = place[0]
    rho = rho_ref[0]
    full = values.shape[1]
    blocks = full // LANES
    half_rows = blocks // 2
    last = edges.shape[0] - 1
    halves = (edges[last].astype(jnp.float32), edges[0].astype(jnp.float32))
    for b in range(blocks):
        zrow_out[:, b * LANES : (b + 1) * LANES] = halves[b // half_rows][b % half_rows : b % half_rows + 1, :]
    live = flags[...] == 0
    z = jnp.where(live, zrow_out[...], 0.0)
    zrow_out[...] = z
    total = rho * jnp.sum(z * z)
    weight[...] = jnp.broadcast_to(z * z, weight.shape)
    far[...] = jnp.broadcast_to(jnp.where(live, values[...], FAR), far.shape)
    own = pl.ds(pl.multiple_of(member * LANES, LANES), LANES)
    own_values = values[:, own]
    own_live = flags[:, own] == 0
    pdi[...] = jnp.broadcast_to(column_of(own_values), (LANES, LANES))
    inv_rho = 1.0 / rho
    depth = 8
    tiles = LANES // 8

    def spread(column):
        return jnp.broadcast_to(column, (8, LANES))

    gap = []
    for g in range(0, tiles, depth):
        di = [pdi[8 * (g + r) : 8 * (g + r) + 8, :] for r in range(depth)]
        low = [jnp.full((8, LANES), 2.0 * FAR, jnp.float32) for _ in range(depth)]
        for b in range(blocks):
            sl = slice(b * LANES, (b + 1) * LANES)
            d = far[:, sl]
            for r in range(depth):
                e = d - di[r]
                dist[8 * (g + r) : 8 * (g + r) + 8, sl] = e
                low[r] = jnp.minimum(low[r], jnp.where(e > 0, e, 2.0 * FAR))
        for r in range(depth):
            least = spread(jnp.min(low[r], axis=1, keepdims=True))
            gap.append(jnp.where(least > 0.5 * FAR, (di[r] + total) - di[r], least))
    for r in range(tiles):
        pdi[8 * r : 8 * r + 8, :] = gap[r]
        pde[8 * r : 8 * r + 8, :] = 0.5 * gap[r]

    def sweep(_, carry):
        for g in range(0, tiles, depth):
            de = [pde[8 * (g + r) : 8 * (g + r) + 8, :] for r in range(depth)]
            f = [jnp.zeros((8, LANES), jnp.float32) for _ in range(depth)]
            h = [jnp.zeros((8, LANES), jnp.float32) for _ in range(depth)]
            for b in range(blocks):
                sl = slice(b * LANES, (b + 1) * LANES)
                w = weight[:, sl]
                for r in range(depth):
                    inverse = pltpu.reciprocal(dist[8 * (g + r) : 8 * (g + r) + 8, sl] - de[r], approx=True)
                    term = w * inverse
                    f[r] = f[r] + term
                    h[r] = h[r] + term * inverse
            for r in range(depth):
                top = inv_rho + spread(jnp.sum(f[r], axis=1, keepdims=True))
                slope = spread(jnp.sum(h[r], axis=1, keepdims=True))
                gp = pdi[8 * (g + r) : 8 * (g + r) + 8, :]
                pde[8 * (g + r) : 8 * (g + r) + 8, :] = jnp.clip(de[r] - top / slope, MARGIN * gp, (1.0 - MARGIN) * gp)
        return carry

    lax.fori_loop(0, ITERS, sweep, 0, unroll=True)
    own_delta = jnp.where(own_live, row_of(pde[...][:, :1]), 0.0)
    eig[...] = own_values + own_delta
    pde[...] = jnp.broadcast_to(column_of(own_delta), (LANES, LANES))
    for b in range(blocks):
        sl = slice(b * LANES, (b + 1) * LANES)
        p = None
        for g in range(0, tiles, 4):
            num = den = None
            for r in range(g, g + 4):
                e = dist[8 * r : 8 * r + 8, sl]
                a = e - pde[8 * r : 8 * r + 8, :]
                c = jnp.where(e == 0, 1.0, e)
                num = a if num is None else num * a
                den = c if den is None else den * c
            ratio = num * pltpu.reciprocal(den, approx=True)
            p = ratio if p is None else p * ratio
        prod[:, sl] = p
    p = prod[...]
    p = p[:4] * p[4:]
    p = p[:2] * p[2:]
    p = p[:1] * p[1:]
    for b in range(blocks):
        out[b : b + 1, :] = p[:, b * LANES : (b + 1) * LANES]
    out[blocks : blocks + 1, :] = own_delta
    out[blocks + 1 :, :] = jnp.zeros((out.shape[0] - blocks - 1, LANES), jnp.float32)


def vectors_kernel(offsets, first, place, rho_ref, parts, values, flags, *refs):
    if first:
        zrow, own, left, right, far0, far1, *outs, zhat, far = refs[:-4]
    else:
        zhat, far, own, left, right, far0, far1, *outs = refs[:-4]
    basis, held, pdi, pde = refs[-4:]
    z, x = place[1], place[2]
    nz, nx = 8, 4
    share = own.shape[1]
    full = values.shape[1]
    half = full // 2
    blocks = full // LANES

    if first:
        p = parts[0, :blocks]
        for s in range(1, parts.shape[0]):
            p = p * parts[s, :blocks]
        p = jnp.sqrt(jnp.abs(p) / rho_ref[0])
        for r in range(blocks):
            zhat[:, r * LANES : (r + 1) * LANES] = jnp.broadcast_to(p[r : r + 1, :], (8, LANES))
        live = flags[...] == 0
        live8 = jnp.broadcast_to(flags[...], far.shape) == 0
        signed = jnp.where(jnp.broadcast_to(zrow[...], far.shape) >= 0, zhat[...], -zhat[...])
        zhat[...] = jnp.where(live8, signed, 0.0)
        far[...] = jnp.broadcast_to(jnp.where(live, values[...], FAR), far.shape)

    places = [lax.rem(z + offset, nz) for offset in offsets]
    owners = [at * nx + x for at in places]
    for k, owner in enumerate(owners):
        cols = pl.ds(pl.multiple_of(owner * LANES, LANES), LANES)
        pdi[k * LANES : (k + 1) * LANES, :] = jnp.broadcast_to(column_of(values[:, cols]), (LANES, LANES))
        pde[k * LANES : (k + 1) * LANES, :] = jnp.broadcast_to(
            column_of(parts[places[k], blocks : blocks + 1, :]), (LANES, LANES)
        )
    depth = 8

    def group(g):
        base = g * 8 * depth
        di = [pdi[pl.ds(base + 8 * r, 8), :] for r in range(depth)]
        de = [pde[pl.ds(base + 8 * r, 8), :] for r in range(depth)]
        acc = [jnp.zeros((8, LANES), jnp.float32) for _ in range(depth)]
        for b in range(blocks):
            sl = slice(b * LANES, (b + 1) * LANES)
            d, zh = far[:, sl], zhat[:, sl]
            for r in range(depth):
                v = zh * pltpu.reciprocal((d - di[r]) - de[r], approx=True)
                acc[r] = acc[r] + v * v
                held[8 * r : 8 * r + 8, sl] = v
        scale = [lax.rsqrt(jnp.sum(a, axis=1, keepdims=True)) for a in acc]
        scale = [jnp.broadcast_to(a, (8, LANES)) for a in scale]
        for b in range(blocks):
            sl = slice(b * LANES, (b + 1) * LANES)
            for r in range(0, depth, 2):
                u = [held[8 * t : 8 * t + 8, sl] * scale[t] for t in (r, r + 1)]
                basis[pl.ds(base + 8 * r, 16), sl] = jnp.concatenate(u, axis=0).astype(jnp.bfloat16)

    for g in range(len(offsets) * LANES // (8 * depth)):
        group(g)
    for c in range(2):
        slots = (own.at[c], left.at[c], right.at[c], (far0, far1)[c])
        lhs = jnp.concatenate([slot[...] for slot in slots], axis=0)
        rhs = basis[:, c * half : (c + 1) * half]
        acc = lax.dot_general(lhs, rhs, (((1,), (1,)), ((), ())), preferred_element_type=jnp.float32)
        for k, owner in enumerate(owners):
            dead = flags[:, pl.ds(pl.multiple_of(owner * LANES, LANES), LANES)] != 0
            mine = owner < blocks // 2 if c == 0 else owner >= blocks // 2
            inner = jnp.where(mine, owner if c == 0 else owner - blocks // 2, 0)
            for s, slot in enumerate(slots):
                plain = slot[:, pl.ds(pl.multiple_of(inner * LANES, LANES), LANES)].astype(jnp.float32)
                plain = jnp.where(mine, plain, 0.0)
                got = acc[s * share : (s + 1) * share, k * LANES : (k + 1) * LANES]
                source = lax.rem(x + (0, nx - 1, 1, 2)[s], nx)
                outs[k][c, pl.ds(pl.multiple_of(source * share, share), share), :] = jnp.where(dead, plain, got).astype(
                    jnp.bfloat16
                )


def local(child_vectors, child_values, deflated, order, coupling):
    del order
    half = child_vectors.shape[2]
    full = 2 * half
    rows = child_vectors.shape[1]
    nz, nx = lax.axis_size("z"), lax.axis_size("x")
    group = nz * nx
    z, x = lax.axis_index("z"), lax.axis_index("x")
    member = z * nx + x
    blocks = full // LANES
    whole = lambda: pl.BlockSpec(memory_space=pltpu.VMEM)
    scalar = lambda: pl.BlockSpec(memory_space=pltpu.SMEM)

    ahead = [(i, (i + 1) % nx) for i in range(nx)]
    back = [(i, (i - 1) % nx) for i in range(nx)]
    left = lax.ppermute(child_vectors, "x", ahead)
    right = lax.ppermute(child_vectors, "x", back)

    place = jnp.stack([member, z, x]).astype(jnp.int32)
    edge = jnp.where(member == group - 1, child_vectors[0, rows - 1], child_vectors[1, 0])
    edge = jnp.broadcast_to(edge.reshape(1, half // LANES, LANES), (group, half // LANES, LANES))
    edges = lax.all_to_all(edge, ("z", "x"), 0, 0, tiled=True)
    child_values, left, right = lax.optimization_barrier((child_values, left, right))
    values = child_values.reshape(1, full)
    flags = deflated.reshape(1, full)
    block, eig, zrow = pl.pallas_call(
        roots_kernel,
        out_shape=(
            jax.ShapeDtypeStruct((blocks + 8, LANES), jnp.float32),
            jax.ShapeDtypeStruct((1, LANES), jnp.float32),
            jax.ShapeDtypeStruct((1, full), jnp.float32),
        ),
        in_specs=[scalar(), scalar(), whole(), whole(), whole()],
        out_specs=(whole(), whole(), whole()),
        scratch_shapes=[
            pltpu.VMEM((8, full), jnp.float32),
            pltpu.VMEM((8, full), jnp.float32),
            pltpu.VMEM((LANES, full), jnp.float32),
            pltpu.VMEM((LANES, LANES), jnp.float32),
            pltpu.VMEM((LANES, LANES), jnp.float32),
            pltpu.VMEM((8, full), jnp.float32),
        ],
        compiler_params=pltpu.CompilerParams(vmem_limit_bytes=32 * 1024 * 1024),
        name="roots",
    )(place, coupling, edges, values, flags)
    others = [lax.ppermute(block, "x", [(i, (i + k) % nx) for i in range(nx)]) for k in (2, 1, 3)]
    left, right, *others = lax.optimization_barrier((left, right, *others))
    opposite = (lax.ppermute(left[0], "x", ahead), lax.ppermute(right[1], "x", back))
    product = block
    for other in others:
        product = product * other
    lines = lax.broadcasted_iota(jnp.int32, block.shape, 0)
    parts = jnp.broadcast_to(jnp.where(lines < blocks, product, block), (nz,) + block.shape)
    parts = lax.all_to_all(parts, "z", 0, 0, tiled=True)
    calls = ((4,), (5, 3), (6, 2), (7, 1), (0,))
    order = sum(calls, ())
    piece = jax.ShapeDtypeStruct((2, nx * rows, LANES), jnp.bfloat16)
    wide = jax.ShapeDtypeStruct((8, full), jnp.float32)
    held = (zrow,)
    pieces = []
    for at, some in enumerate(calls):
        wait = {3: 0, 4: 1}.get(at)
        if wait is not None:
            pieces[wait], *held = lax.optimization_barrier((pieces[wait], *held))
        extra = (wide, wide) if at == 0 else ()
        *made, = pl.pallas_call(
            functools.partial(vectors_kernel, some, at == 0),
            out_shape=(piece,) * len(some) + extra,
            in_specs=[scalar(), scalar()] + [whole()] * (8 + len(held)),
            out_specs=(whole(),) * (len(some) + len(extra)),
            scratch_shapes=[
                pltpu.VMEM((len(some) * LANES, full), jnp.bfloat16),
                pltpu.VMEM((64, full), jnp.float32),
                pltpu.VMEM((len(some) * LANES, LANES), jnp.float32),
                pltpu.VMEM((len(some) * LANES, LANES), jnp.float32),
            ],
            compiler_params=pltpu.CompilerParams(vmem_limit_bytes=24 * 1024 * 1024),
            name="vectors",
        )(place, coupling, parts, values, flags, *held, child_vectors, left, right, *opposite)
        if at == 0:
            held = tuple(made[len(some) :])
        for offset, block in zip(some, made):
            if offset:
                block = lax.ppermute(block, "z", [(i, (i + offset) % nz) for i in range(nz)])
            pieces.append(block)
    pieces = lax.optimization_barrier(pieces[::-1])[::-1]
    eigenvectors = jnp.zeros((2, nz, nx * rows, LANES), jnp.bfloat16)
    for offset, block in zip(order, pieces):
        source = lax.rem(z + nz - offset, nz)
        eigenvectors = lax.dynamic_update_slice(eigenvectors, block[:, None], (0, source, 0, 0))
    eigenvectors = eigenvectors.reshape(full, LANES)
    return eig.reshape(LANES), eigenvectors


def solution(mesh):
    inner = Mesh(mesh.devices.reshape(mesh.devices.shape[0], -1, 4), ("merge", "z", "x"))
    grp = ("z", "x")
    in_specs = (P("merge", grp, None), P("merge"), P("merge"), P("merge"), P("merge"))
    out_specs = (P(("merge",) + grp), P("merge", grp))
    return jax.shard_map(local, mesh=inner, in_specs=in_specs, out_specs=out_specs, check_vma=False)
```
